32 devices in a mesh: section: 4 (over x, core), dp: 8 (over z, y).
Axes of the slice: x: 2, y: 2, z: 4, core: 2. Of those that a mesh axis runs over, the one named last changes fastest.
Arguments:
- acts: bfloat16 [4, 3072, 4096], P('section', 'dp'), may hold values from -6 to 6
- cotangent: bfloat16 [3072, 4096], P('dp'), may hold values from -6 to 6
- gains: float32 [4, 4096], P('section'), may hold values from 0.1 to 1.9
- value_w: bfloat16 [4, 4096, 1024], P('section', 'dp'), may hold values from -0.09375 to 0.09375
- output_w: bfloat16 [4, 1024, 4096], P('section', None, 'dp'), may hold values from -0.1875 to 0.1875
- d_map: int32 [4, 64], P('section'), may hold values from 0 to 3
- r_map: int32 [4, 16], P('section'), may hold values from 0 to 3
- lengths: int32 [24], P('dp'), may hold values from 32 to 128, as said below
- item_panels: bfloat16 [8, 4, 2, 128, 128], P('dp', 'section'), may hold values from -24 to 24
- owners: int32 [8], replicated, may hold values from 0 to 7, each once
Outputs:
- grad_in: bfloat16 [4, 3072, 4096], P('section', 'dp')
- scores: float32 [24, 8], P('dp')
The draws below stay inside these ranges and needn't reach their ends.
Inputs may be any that keep to these rules, and one draw needn't show every extreme that they name: `lengths`: some document is fully live (128 tokens) in every draw.
All inputs are finite; a program needn't handle non-finite values.
Results may differ from the reference program's by a relative error of at most 0.015.
Values may be sent and summed in bfloat16 or wider, within the bound.
A program may use at most 128 MiB of HBM per device.

```python
import jax
import jax.numpy as jnp
from jax import lax

D = 4096
R = 1024
BLOCK = 64
DBINS = 2
RBINS = 2
DOC_LEN = 128
ITEM_DEV = 1
TOKENS = 3072
DOCS = 24
ITEMS = 8
DBLOCKS = 64
RBLOCKS = 16
KD = 128
KR = 128
N_SECTION = 4
N_DP = 8


def draw_lengths(key, part):
    drawn = jax.random.randint(key, (DOCS,), DOC_LEN // 4, DOC_LEN + 1, dtype=jnp.int32)
    slots = jnp.arange(DOCS, dtype=jnp.int32)
    drawn = jnp.where(slots == 0, DOC_LEN, drawn)
    return jnp.where(slots == DOCS - 1, DOC_LEN // 4, drawn)


def touch_ends(result, key, least, top_value):
    shape = result.shape
    spot = [jax.random.randint(jax.random.fold_in(key, axis), (), 0, shape[axis]) for axis in range(len(shape))]
    result = result.at[tuple(spot)].set(least)
    longest = shape.index(max(shape))
    spot[longest] = (spot[longest] + 1) % shape[longest]
    return result.at[tuple(spot)].set(top_value)


def block_levels(key, shape, shards, least, top_value):
    gain, own = 1.0, jax.random.fold_in(key, 6)
    for dim, parts in shards:
        draws = jnp.exp(jax.random.uniform(jax.random.fold_in(own, dim), (parts,), jnp.float32, least / len(shards), top_value / len(shards)))
        gain = gain * jnp.repeat(draws, shape[dim] // parts).reshape([-1 if axis == dim else 1 for axis in range(len(shape))])
    return gain


def gaussian(stream_key, shape, spread, most, cuts=(), kind=jnp.bfloat16):
    result = jax.random.normal(stream_key, shape, jnp.float32) * spread
    if len(cuts) > 0:
        result = block_levels(stream_key, shape, cuts, -0.22, 0.18) * result
    return jnp.clip(result, min=-most, max=most).astype(kind)


def setup_inputs(seed: int = 0) -> dict:
    keys = jax.random.split(jax.random.key(seed), 11)
    acts = gaussian(keys[0], (N_SECTION, TOKENS, D), 1.0, 6.0, ((0, 4), (1, 8)))
    cotangent = gaussian(keys[1], (TOKENS, D), 1.0, 6.0, ((0, 8),))
    gains = jnp.clip(1.0 + 0.18 * jax.random.normal(keys[2], (N_SECTION, D), jnp.float32), 0.1, 1.9)
    value_w = gaussian(keys[3], (N_SECTION, D, R), D ** -0.5, 0.09375, ((0, 4), (1, 8)))
    output_w = gaussian(keys[4], (N_SECTION, R, D), R ** -0.5, 0.1875, ((0, 4), (2, 8)))
    d_map = touch_ends(jax.random.randint(keys[5], (N_SECTION, DBLOCKS), 0, 2 * DBINS), jax.random.fold_in(keys[5], 1), 0, (2 * DBINS) - 1).astype(jnp.int32)
    r_map = touch_ends(jax.random.randint(keys[6], (N_SECTION, RBLOCKS), 0, 2 * RBINS), jax.random.fold_in(keys[6], 1), 0, (2 * RBINS) - 1).astype(jnp.int32)
    lengths = draw_lengths(jax.random.fold_in(keys[10], 71), 0)
    item_panels = gaussian(keys[8], (ITEMS, N_SECTION, 2, KD, KR), 4.0, 24.0, ((0, 8), (1, 4)))
    owners = jax.random.permutation(keys[9], N_DP).astype(jnp.int32)
    return dict(acts=acts, cotangent=cotangent, gains=gains, value_w=value_w, output_w=output_w, d_map=d_map, r_map=r_map, lengths=lengths, item_panels=item_panels, owners=owners)


def normalize(inputs, gain_row):
    return inputs * lax.rsqrt(lax.optimization_barrier(jnp.mean(inputs * inputs, axis=-1, keepdims=True)) + 1e-05) * gain_row

def sketch_matrix(codes, bin_count):
    levels = jnp.arange(bin_count, dtype=jnp.int32)
    sign_row = (1 - 2 * (codes // bin_count)).astype(jnp.float32)
    return jnp.where(levels[:, None] == (codes % bin_count)[None, :], sign_row[None, :], jnp.zeros_like(sign_row)[None, :])

def project_rows(values, sketch):
    row_count = values.shape[0]
    block_count = values.shape[1] // BLOCK
    bin_count = sketch.shape[0]
    pieces = values.astype(jnp.float32).reshape(row_count, block_count, BLOCK)
    mapped = jnp.einsum('tbc,kb->tkc', pieces, sketch, precision=lax.Precision.HIGHEST)
    return mapped.reshape(row_count, bin_count * BLOCK) * (block_count / bin_count) ** (-0.5)

def reference(acts, cotangent, gains, value_w, output_w, d_map, r_map, lengths, item_panels, owners):
    positions = jnp.arange(DOC_LEN, dtype=jnp.int32)
    live_mask = (positions[None, :] < lengths[:, None]).reshape(TOKENS, 1)
    current = jnp.where(live_mask, cotangent, jnp.zeros_like(cotangent))
    feature_width = 2 * KD * KR
    ordered = item_panels.reshape(N_DP, ITEM_DEV, N_SECTION, feature_width)[owners].reshape(ITEMS, N_SECTION, feature_width)
    inverse_len = 1.0 / lengths.astype(jnp.float32)
    scores = jnp.zeros((DOCS, ITEMS), jnp.float32)
    outputs = []
    for section in range(N_SECTION - 1, -1, -1):
        inputs = acts[section].astype(jnp.float32)
        gain_row = gains[section]
        hidden = normalize(inputs, gain_row).astype(jnp.bfloat16)
        values = jnp.dot(hidden, value_w[section], preferred_element_type=jnp.float32).astype(jnp.bfloat16)
        dvalues = jnp.dot(current, output_w[section].T, preferred_element_type=jnp.float32).astype(jnp.bfloat16)
        dhidden = jnp.dot(dvalues, value_w[section].T, preferred_element_type=jnp.float32)
        _, pullback = jax.vjp(lambda probe: normalize(probe, gain_row), inputs)
        grad_next = (current.astype(jnp.float32) + pullback(dhidden)[0]).astype(jnp.bfloat16)
        model_sketch = sketch_matrix(d_map[section], DBINS)
        value_sketch = sketch_matrix(r_map[section], RBINS)
        hidden_proj = project_rows(hidden, model_sketch).reshape(DOCS, DOC_LEN, KD)
        dvalue_proj = project_rows(dvalues, value_sketch).reshape(DOCS, DOC_LEN, KR)
        grad_proj = project_rows(current, model_sketch).reshape(DOCS, DOC_LEN, KD)
        value_proj = project_rows(values, value_sketch).reshape(DOCS, DOC_LEN, KR)
        first_feat = jnp.einsum('dtk,dtj->dkj', hidden_proj, dvalue_proj, precision=lax.Precision.HIGHEST)
        second_feat = jnp.einsum('dtk,dtj->dkj', grad_proj, value_proj, precision=lax.Precision.HIGHEST)
        features = jnp.stack([first_feat, second_feat], axis=1) * inverse_len[:, None, None, None]
        features = features.reshape(DOCS, feature_width).astype(jnp.bfloat16)
        scores = scores + jnp.dot(features, ordered[:, section].T, preferred_element_type=jnp.float32)
        outputs.insert(0, grad_next)
        current = grad_next
    return (jnp.stack(outputs), scores * (KD * KR) ** (-0.5))
```

```python
import jax
import jax.numpy as jnp
from jax import lax
from jax.sharding import PartitionSpec as P

BLOCK = 64
DBINS = 2
RBINS = 2
EPS = 1e-05


def projection(codes, bin_count):
    width = codes.shape[0] * BLOCK
    row_codes = jnp.repeat(codes, BLOCK)[:, None]
    shape = (width, bin_count * BLOCK)
    rows = lax.broadcasted_iota(jnp.int32, shape, 0)
    cols = lax.broadcasted_iota(jnp.int32, shape, 1)
    hit = (rows % BLOCK == cols % BLOCK) & (row_codes % bin_count == cols // BLOCK)
    sign = 1 - 2 * (row_codes // bin_count)
    return jnp.where(hit, sign, 0).astype(jnp.bfloat16)


def project_rows(values, matrix, bin_count):
    scale = (values.shape[1] // BLOCK / bin_count) ** (-0.5)
    return jnp.dot(values, matrix, preferred_element_type=jnp.float32) * scale


def gather_weights(value_w, output_w):
    return (
        lax.all_gather(value_w, "dp", axis=0, tiled=True),
        lax.all_gather(output_w, "dp", axis=1, tiled=True),
    )


def chain_step(current, inputs_bf, inv_rms, values, gain_row, value_full, output_full):
    dvalues = lax.dot_general(
        current, output_full, (((1,), (1,)), ((), ())), preferred_element_type=jnp.float32
    ).astype(jnp.bfloat16)
    row_sum = jnp.sum(dvalues.astype(jnp.float32) * values, axis=-1, keepdims=True)
    dhidden = lax.dot_general(
        dvalues, value_full, (((1,), (1,)), ((), ())), preferred_element_type=jnp.float32
    )
    coef = row_sum * inv_rms * inv_rms / inputs_bf.shape[1]
    grad_next = (
        current.astype(jnp.float32)
        + dhidden * gain_row * inv_rms
        - inputs_bf.astype(jnp.float32) * coef
    ).astype(jnp.bfloat16)
    return dvalues, grad_next


def body(acts, cotangent, gains, value_w, output_w, d_map, r_map, lengths, item_panels, owners):
    section_count = lax.axis_size("section")
    section_id = lax.axis_index("section")
    last_section = section_count - 1
    owner_count = lax.axis_size("dp")
    dp_id = lax.axis_index("dp")
    doc_count = lengths.shape[0]
    inputs_bf = acts[0]
    token_count, model_width = inputs_bf.shape
    slot_count = token_count // doc_count
    feature_width = item_panels.shape[2] * item_panels.shape[3] * item_panels.shape[4]

    value_full, output_full = gather_weights(value_w[0], output_w[0])

    own_panels = item_panels[:, 0].reshape(item_panels.shape[0], feature_width)
    per_owner = own_panels.shape[0]
    panels = [own_panels]
    for distance in range(1, owner_count):
        route = [(i, (i + distance) % owner_count) for i in range(owner_count)]
        panels.append(lax.ppermute(own_panels, "dp", route))
    all_rows = jnp.concatenate(panels, axis=0)

    gain_row = gains
    inputs = inputs_bf.astype(jnp.float32)
    inv_rms = lax.rsqrt(jnp.mean(inputs * inputs, axis=-1, keepdims=True) + EPS)
    hidden = (inputs * inv_rms * gain_row).astype(jnp.bfloat16)
    model_matrix = projection(d_map[0], DBINS)
    value_matrix = projection(r_map[0], RBINS)
    hidden_proj = project_rows(hidden, model_matrix, DBINS)
    values = jnp.dot(hidden, value_full, preferred_element_type=jnp.float32)
    value_proj = project_rows(values.astype(jnp.bfloat16), value_matrix, RBINS)

    positions = jnp.arange(slot_count, dtype=jnp.int32)
    live_mask = (positions[None, :] < lengths[:, None]).reshape(token_count, 1)
    current = jnp.where(live_mask, cotangent, jnp.zeros_like(cotangent))

    for turn in range(section_count):
        dvalues, grad_next = chain_step(
            current, inputs_bf, inv_rms, values, gain_row, value_full, output_full
        )
        if turn < last_section:
            source = last_section - turn
            incoming = lax.ppermute(grad_next, "section", [(source, source - 1)])
            current = jnp.where(section_id == source - 1, incoming, current)

    dvalue_proj = project_rows(dvalues, value_matrix, RBINS)
    grad_proj = project_rows(current, model_matrix, DBINS)

    def by_doc(rows):
        return rows.reshape(doc_count, slot_count, rows.shape[1])

    def feature(left, right):
        return jnp.einsum(
            "dtk,dtj->dkj", by_doc(left), by_doc(right), precision=lax.Precision.HIGHEST
        )

    inverse_len = 1.0 / lengths.astype(jnp.float32)
    features = jnp.stack(
        [feature(hidden_proj, dvalue_proj), feature(grad_proj, value_proj)], axis=1
    )
    features = (features * inverse_len[:, None, None, None]).astype(jnp.bfloat16)
    features = features.reshape(doc_count, feature_width)
    products = lax.dot_general(
        features, all_rows, (((1,), (1,)), ((), ())), preferred_element_type=jnp.float32
    )
    places = jnp.mod(dp_id - owners, owner_count)
    collected = jnp.take(
        products.reshape(doc_count, owner_count, per_owner), places, axis=1
    ).reshape(doc_count, owner_count * per_owner)
    scores = lax.psum(collected * (feature_width // 2) ** (-0.5), "section")
    return (grad_next[None], scores)


def solution(mesh):
    in_specs = (
        P("section", "dp", None),
        P("dp", None),
        P("section", None),
        P("section", "dp", None),
        P("section", None, "dp"),
        P("section", None),
        P("section", None),
        P("dp"),
        P("dp", "section", None, None, None),
        P(),
    )
    out_specs = (P("section", "dp", None), P("dp", None))
    return jax.shard_map(body, mesh=mesh, in_specs=in_specs, out_specs=out_specs, check_vma=False)
```

```python
import functools

import jax
import jax.numpy as jnp
from jax import lax
from jax.experimental import pallas as pl
from jax.experimental.pallas import tpu as pltpu
from jax.sharding import PartitionSpec as P

BLOCK = 64
DBINS = 2
RBINS = 2
EPS = 1e-05


def projection(codes, bin_count):
    width = codes.shape[0] * BLOCK
    row_codes = jnp.repeat(codes, BLOCK)[:, None]
    shape = (width, bin_count * BLOCK)
    rows = lax.broadcasted_iota(jnp.int32, shape, 0)
    cols = lax.broadcasted_iota(jnp.int32, shape, 1)
    hit = (rows % BLOCK == cols % BLOCK) & (row_codes % bin_count == cols // BLOCK)
    sign = 1 - 2 * (row_codes // bin_count)
    return jnp.where(hit, sign, 0).astype(jnp.bfloat16)


def project_rows(values, matrix, bin_count):
    scale = (values.shape[1] // BLOCK / bin_count) ** (-0.5)
    return jnp.dot(values, matrix, preferred_element_type=jnp.float32) * scale


def gather_kernel(
    line, value_ref, output_ref, value_full, output_full, local_sem, send_sem, recv_sem
):
    me = lax.axis_index("dp")
    place = me // 2
    side = me % 2
    partner = place * 2 + (1 - side)
    has_left = place > 0
    has_right = place < line - 1
    depth = value_ref.shape[0]
    width = output_ref.shape[1]

    barrier = pltpu.get_barrier_semaphore()

    def greet(device):
        pl.semaphore_signal(
            barrier, inc=1, device_id={"dp": device}, device_id_type=pl.DeviceIdType.MESH
        )

    greet(partner)

    @pl.when(has_left)
    def _():
        greet(me - 2)

    @pl.when(has_right)
    def _():
        greet(me + 2)

    peers = 1 + has_left.astype(jnp.int32) + has_right.astype(jnp.int32)
    pl.semaphore_wait(barrier, peers)

    def slot(weight, block):
        if weight == 0:
            if len(output_full.shape) == 3:
                return output_full.at[block]
            return output_full.at[:, pl.ds(pl.multiple_of(block * width, width), width)]
        return value_full.at[pl.ds(pl.multiple_of(block * depth, depth), depth), :]

    def copy(weight, block, device, way, own):
        source = (output_ref, value_ref)[weight] if own else slot(weight, block)
        return pltpu.make_async_remote_copy(
            src_ref=source,
            dst_ref=slot(weight, block),
            send_sem=send_sem.at[weight, way, block // 2],
            recv_sem=recv_sem.at[weight, block],
            device_id={"dp": device},
            device_id_type=pl.DeviceIdType.MESH,
        )

    def local(weight):
        return pltpu.make_async_copy(
            (output_ref, value_ref)[weight], slot(weight, me), local_sem.at[weight]
        )

    for weight in range(2):

        @pl.when(has_left)
        def _():
            copy(weight, me, me - 2, 0, True).start()

        @pl.when(has_right)
        def _():
            copy(weight, me, me + 2, 1, True).start()

        copy(weight, me, partner, 2, True).start()
        local(weight).start()

    def relay(step, carry):
        for weight in range(2):
            from_left = me - 2 * step
            from_right = me + 2 * step

            @pl.when(place + step < line)
            def _():
                copy(weight, from_right, partner, 2, False).wait_recv()

                @pl.when(has_left)
                def _():
                    copy(weight, from_right, me - 2, 0, False).start()

                copy(weight, from_right, partner, 2, False).start()

            @pl.when(place - step >= 0)
            def _():
                copy(weight, from_left, partner, 2, False).wait_recv()

                @pl.when(has_right)
                def _():
                    copy(weight, from_left, me + 2, 1, False).start()

                copy(weight, from_left, partner, 2, False).start()

        return carry

    lax.fori_loop(1, line, relay, 0)

    def finish(index, carry):
        for weight in range(2):
            mine = index * 2 + side
            copy(weight, index * 2 + (1 - side), partner, 2, False).wait_recv()
            copy(weight, mine, partner, 2, False).wait_send()

            @pl.when(has_left & (index >= place))
            def _():
                copy(weight, mine, partner, 0, False).wait_send()

            @pl.when(has_right & (index <= place))
            def _():
                copy(weight, mine, partner, 1, False).wait_send()

        return carry

    lax.fori_loop(0, line, finish, 0)
    for weight in range(2):
        local(weight).wait()


def gather_weights(value_w, output_w):
    count = lax.axis_size("dp")
    line = count // 2
    rows, width = output_w.shape
    aligned = width % 128 == 0
    output_shape = (rows, width * count) if aligned else (count, rows, width)
    value_full, output_full = pl.pallas_call(
        functools.partial(gather_kernel, line),
        out_shape=(
            jax.ShapeDtypeStruct((value_w.shape[0] * count, value_w.shape[1]), value_w.dtype),
            jax.ShapeDtypeStruct(output_shape, output_w.dtype),
        ),
        in_specs=[pl.BlockSpec(memory_space=pl.ANY)] * 2,
        out_specs=(pl.BlockSpec(memory_space=pl.ANY), pl.BlockSpec(memory_space=pl.ANY)),
        scratch_shapes=[
            pltpu.SemaphoreType.DMA((2,)),
            pltpu.SemaphoreType.DMA((2, 3, line)),
            pltpu.SemaphoreType.DMA((2, count)),
        ],
        compiler_params=pltpu.CompilerParams(collective_id=0, has_side_effects=True),
        name="gather_weights",
    )(value_w, output_w)
    if not aligned:
        output_full = output_full.swapaxes(0, 1).reshape(rows, width * count)
    return value_full, output_full


def chain_step(current, inputs_bf, inv_rms, values, gain_row, value_full, output_full):
    dvalues = lax.dot_general(
        current, output_full, (((1,), (1,)), ((), ())), preferred_element_type=jnp.float32
    ).astype(jnp.bfloat16)
    row_sum = jnp.sum(dvalues.astype(jnp.float32) * values, axis=-1, keepdims=True)
    dhidden = lax.dot_general(
        dvalues, value_full, (((1,), (1,)), ((), ())), preferred_element_type=jnp.float32
    )
    coef = row_sum * inv_rms * inv_rms / inputs_bf.shape[1]
    grad_next = (
        current.astype(jnp.float32)
        + dhidden * gain_row * inv_rms
        - inputs_bf.astype(jnp.float32) * coef
    ).astype(jnp.bfloat16)
    return dvalues, grad_next


def body(acts, cotangent, gains, value_w, output_w, d_map, r_map, lengths, item_panels, owners):
    section_count = lax.axis_size("section")
    section_id = lax.axis_index("section")
    last_section = section_count - 1
    owner_count = lax.axis_size("dp")
    dp_id = lax.axis_index("dp")
    doc_count = lengths.shape[0]
    inputs_bf = acts[0]
    token_count, model_width = inputs_bf.shape
    slot_count = token_count // doc_count
    feature_width = item_panels.shape[2] * item_panels.shape[3] * item_panels.shape[4]

    value_full, output_full = gather_weights(value_w[0], output_w[0])

    own_panels = item_panels[:, 0].reshape(item_panels.shape[0], feature_width)
    per_owner = own_panels.shape[0]
    panels = [own_panels]
    for distance in range(1, owner_count):
        route = [(i, (i + distance) % owner_count) for i in range(owner_count)]
        panels.append(lax.ppermute(own_panels, "dp", route))
    all_rows = jnp.concatenate(panels, axis=0)

    gain_row = gains
    inputs = inputs_bf.astype(jnp.float32)
    inv_rms = lax.rsqrt(jnp.mean(inputs * inputs, axis=-1, keepdims=True) + EPS)
    hidden = (inputs * inv_rms * gain_row).astype(jnp.bfloat16)
    model_matrix = projection(d_map[0], DBINS)
    value_matrix = projection(r_map[0], RBINS)
    hidden_proj = project_rows(hidden, model_matrix, DBINS)
    values = jnp.dot(hidden, value_full, preferred_element_type=jnp.float32)
    value_proj = project_rows(values.astype(jnp.bfloat16), value_matrix, RBINS)

    positions = jnp.arange(slot_count, dtype=jnp.int32)
    live_mask = (positions[None, :] < lengths[:, None]).reshape(token_count, 1)
    current = jnp.where(live_mask, cotangent, jnp.zeros_like(cotangent))

    for turn in range(section_count):
        dvalues, grad_next = chain_step(
            current, inputs_bf, inv_rms, values, gain_row, value_full, output_full
        )
        if turn < last_section:
            source = last_section - turn
            incoming = lax.ppermute(grad_next, "section", [(source, source - 1)])
            current = jnp.where(section_id == source - 1, incoming, current)

    dvalue_proj = project_rows(dvalues, value_matrix, RBINS)
    grad_proj = project_rows(current, model_matrix, DBINS)

    def by_doc(rows):
        return rows.reshape(doc_count, slot_count, rows.shape[1])

    def feature(left, right):
        return jnp.einsum(
            "dtk,dtj->dkj", by_doc(left), by_doc(right), precision=lax.Precision.HIGHEST
        )

    inverse_len = 1.0 / lengths.astype(jnp.float32)
    features = jnp.stack(
        [feature(hidden_proj, dvalue_proj), feature(grad_proj, value_proj)], axis=1
    )
    features = (features * inverse_len[:, None, None, None]).astype(jnp.bfloat16)
    features = features.reshape(doc_count, feature_width)
    products = lax.dot_general(
        features, all_rows, (((1,), (1,)), ((), ())), preferred_element_type=jnp.float32
    )
    places = jnp.mod(dp_id - owners, owner_count)
    collected = jnp.take(
        products.reshape(doc_count, owner_count, per_owner), places, axis=1
    ).reshape(doc_count, owner_count * per_owner)
    scores = lax.psum(collected * (feature_width // 2) ** (-0.5), "section")
    return (grad_next[None], scores)


def solution(mesh):
    in_specs = (
        P("section", "dp", None),
        P("dp", None),
        P("section", None),
        P("section", "dp", None),
        P("section", None, "dp"),
        P("section", None),
        P("section", None),
        P("dp"),
        P("dp", "section", None, None, None),
        P(),
    )
    out_specs = (P("section", "dp", None), P("dp", None))
    return jax.shard_map(body, mesh=mesh, in_specs=in_specs, out_specs=out_specs, check_vma=False)
```
